512 devices in a mesh: dp: 8 (over x, y_lo), fsdp: 64 (over y_hi, z, core).
Axes of the slice: x: 4, y: 4 (y_hi: 2, y_lo: 2; y = y_hi * 2 + y_lo), z: 16, core: 2. Of those that a mesh axis runs over, the one named last changes fastest.
Arguments:
- tokens: bfloat16 [3072, 4096], P(('dp', 'fsdp')), may hold values from -24 to 24
- w_gate: bfloat16 [4096, 16384], P('dp', 'fsdp'), may hold values from -0.09375 to 0.09375
- w_up: bfloat16 [4096, 16384], P('dp', 'fsdp'), may hold values from -0.09375 to 0.09375
- probe_gate: bfloat16 [4096, 16384], P('dp', 'fsdp'), may hold values from -0.09375 to 0.09375
- probe_up: bfloat16 [4096, 16384], P('dp', 'fsdp'), may hold values from -0.09375 to 0.09375
- w_down: bfloat16 [16384, 4096], P('fsdp', 'dp'), may hold values from -0.09375 to 0.09375
- out_grad: bfloat16 [3072, 4096], P(('dp', 'fsdp')), may hold values from -6 to 6
Outputs:
- hvp_gate: float32 [4096, 16384], P('dp', 'fsdp')
- hvp_up: float32 [4096, 16384], P('dp', 'fsdp')
The draws below stay inside these ranges and needn't reach their ends.
All inputs are finite; a program needn't handle non-finite values.
Results may differ from the reference program's by a relative error of at most 0.015.
Values may be sent and summed in bfloat16 or wider, within the bound.
A program may use at most 64 MiB of HBM per device.

```python
import jax
import jax.numpy as jnp
from jax import lax

D = 4096
H = 16384
TOKENS = 3072
N_DP = 8


def spiked(values, own_key, source, target, shards_of, factor):
    def block_of(position):
        return (jnp.arange(values.shape[position]) // (values.shape[position] // shards_of)).reshape((-1,) + (1,) * (values.ndim - 1 - position))

    one_side = jax.random.permutation(own_key, shards_of)[block_of(target)]
    second = (block_of(target) + shards_of // 2) % shards_of
    return jnp.where((block_of(source) == one_side) | (block_of(source) == second), factor * values, values)


def steps_of(rng, extent, pieces, low, largest):
    def one(axis_at, parts):
        steps = jax.random.uniform(jax.random.fold_in(jax.random.fold_in(rng, 6), axis_at), (parts,), jnp.float32, low / len(pieces), largest / len(pieces))
        return jnp.repeat(jnp.exp(steps), extent[axis_at] // parts).reshape((-1,) + (1,) * (len(extent) - axis_at - 1))

    loudness = one(*pieces[0])
    for cut in pieces[1:]:
        loudness = loudness * one(*cut)
    return loudness


def bell_draw(own_key, dims, width, limit, split=(), kind=jnp.bfloat16):
    drawn = width * jax.random.normal(own_key, dims, jnp.float32)
    if split:
        drawn = drawn * steps_of(own_key, dims, split, -0.22, 0.18)
    return jnp.clip(drawn, -limit, limit).astype(kind)


def noise_with(rng, extent, width, most, split, heavy, dtype=jnp.bfloat16):
    drawn = width * jax.random.normal(rng, extent, jnp.float32)
    if split:
        drawn = drawn * steps_of(rng, extent, split, -0.22, 0.18)
    return jnp.clip(spiked(drawn, jax.random.fold_in(rng, 3), *heavy), -most, most).astype(dtype)


def setup_inputs(seed: int = 0) -> dict:
    splits = jax.random.split(jax.random.key(seed), 8)
    return {
        "tokens": noise_with(splits[0], (TOKENS, D), 1.0, 24.0, ((0, 512),), (0, 1, 512, 6.0)),
        "w_gate": bell_draw(splits[1], (D, H), D ** -0.5, 0.09375, ((0, 8), (1, 64))),
        "w_up": bell_draw(splits[2], (D, H), D ** -0.5, 0.09375, ((0, 8), (1, 64))),
        "probe_gate": bell_draw(splits[3], (D, H), D ** -0.5, 0.09375, ((0, 8), (1, 64))),
        "probe_up": bell_draw(splits[4], (D, H), D ** -0.5, 0.09375, ((0, 8), (1, 64))),
        "w_down": bell_draw(splits[5], (H, D), D ** -0.5, 0.09375, ((0, 64), (1, 8))),
        "out_grad": bell_draw(splits[6], (TOKENS, D), 1.0, 6.0, ((0, 512),)),
    }


def normalize(tokens):
    values = tokens.astype(jnp.float32)
    return (values * lax.rsqrt(lax.optimization_barrier(jnp.mean(values * values, axis=1, keepdims=True)) + 1e-05)).astype(jnp.bfloat16)

def group_term(normed, grads, w_gate, w_up, probe_gate, probe_up, w_down, scale):
    gate = jnp.dot(normed, w_gate, preferred_element_type=jnp.float32)
    up = jnp.dot(normed, w_up, preferred_element_type=jnp.float32)
    tgate = jnp.dot(normed, probe_gate, preferred_element_type=jnp.float32)
    tup = jnp.dot(normed, probe_up, preferred_element_type=jnp.float32)
    dhid = lax.dot_general(grads, w_down, (((1,), (1,)), ((), ())), preferred_element_type=jnp.float32) * scale
    sig = jax.nn.sigmoid(gate)
    first = sig * (1.0 + gate * (1.0 - sig))
    second = sig * (1.0 - sig) * (2.0 + gate * (1.0 - 2.0 * sig))
    left = (dhid * (tup * first + up * second * tgate)).astype(jnp.bfloat16)
    right = (dhid * first * tgate).astype(jnp.bfloat16)
    part_gate = lax.dot_general(normed, left, (((0,), (0,)), ((), ())), preferred_element_type=jnp.float32)
    part_up = lax.dot_general(normed, right, (((0,), (0,)), ((), ())), preferred_element_type=jnp.float32)
    return (part_gate, part_up)

def reference(tokens, w_gate, w_up, probe_gate, probe_up, w_down, out_grad):
    per_group = TOKENS // N_DP
    scale = 1.0 / float(TOKENS) ** 0.5
    tok_blocks = tokens.reshape(N_DP, per_group, tokens.shape[1])
    grad_blocks = out_grad.reshape(N_DP, per_group, out_grad.shape[1])

    def step(carry, pair):
        normed = normalize(pair[0])
        part_gate, part_up = group_term(normed, pair[1], w_gate, w_up, probe_gate, probe_up, w_down, scale)
        part_gate = lax.optimization_barrier(part_gate.astype(jnp.bfloat16)).astype(jnp.float32)
        part_up = lax.optimization_barrier(part_up.astype(jnp.bfloat16)).astype(jnp.float32)
        return ((carry[0] + part_gate, carry[1] + part_up), None)
    start = (jnp.zeros(w_gate.shape, jnp.float32), jnp.zeros(w_up.shape, jnp.float32))
    totals, unused = lax.scan(step, start, (tok_blocks, grad_blocks))
    return (totals[0], totals[1])
```

```python
import functools

import jax
import jax.numpy as jnp
from jax import lax
from jax.experimental import pallas as pl
from jax.experimental.pallas import tpu as pltpu
from jax.sharding import PartitionSpec as P

MESH = pl.DeviceIdType.MESH
F32, BF16 = jnp.float32, jnp.bfloat16

NX, NY, NZ, NC = 4, 2, 16, 2
PEERS = NX * NY * NC
ROWS = 6
BLOCK = PEERS * ROWS
SLICE = 512
PAIRS = NZ // 2
UNIT = 2 * BLOCK
SHARE = UNIT // NX
STACK = 5 * SHARE
TOP = 128
HB = 128
LAG = 4


def kernel(
    blocks,
    scale,
    tokens,
    w_gate,
    w_up,
    probe_gate,
    probe_up,
    w_down,
    grads,
    out_gate,
    out_up,
    both,
    parcels,
    landed,
    tok,
    wide,
    down,
    part,
    via_left,
    via_right,
    from_left,
    from_right,
    tq,
    total,
    half_out,
    half_in,
    a2a_s,
    a2a_r,
    z_s,
    z_r,
    c_s,
    c_r,
    w_l,
    w_s,
    w_r,
    x_s,
    x_r,
    o_s,
    o_r,
):
    dp, fsdp = lax.axis_index("dp"), lax.axis_index("fsdp")
    x, yl = dp // 2, dp % 2
    yh, z, c = fsdp // 32, (fsdp // 2) % NZ, fsdp % 2
    units = blocks * PAIRS

    def device(x_, yl_, yh_, z_, c_):
        return (x_ * 2 + yl_, yh_ * 32 + z_ * 2 + c_)

    xr, xl, xo = (x + 1) % NX, (x + 3) % NX, (x + 2) % NX
    zr, zl = (z + 1) % NZ, (z + NZ - 1) % NZ
    right, left = device(xr, yl, yh, z, c), device(xl, yl, yh, z, c)
    above, below = device(x, yl, yh, zr, c), device(x, yl, yh, zl, c)
    other = device(x, yl, yh, z, 1 - c)
    mate = device(x, 1 - yl, yh, z, c)
    me = x * 4 + yh * 2 + c

    def peer(index):
        return device(index // 4, yl, (index // 2) % 2, z, index % 2)

    def remote(src, dst, send, recv, to):
        return pltpu.make_async_remote_copy(
            src_ref=src, dst_ref=dst, send_sem=send, recv_sem=recv, device_id=to, device_id_type=MESH
        )

    barrier = pltpu.get_barrier_semaphore()

    def greet(k, carry):
        pl.semaphore_signal(barrier, inc=1, device_id=peer((me + k) % PEERS), device_id_type=MESH)
        return carry

    lax.fori_loop(1, PEERS, greet, 0)
    for to in (above, below, mate):
        pl.semaphore_signal(barrier, inc=1, device_id=to, device_id_type=MESH)

    mats = (w_gate, w_up, probe_gate, probe_up)

    def weight_parts(j, slot):
        cols = pl.ds(j * HB, HB)
        pairs = [(m.at[:, cols], wide.at[slot, j, :, pl.ds(i * HB, HB)]) for i, m in enumerate(mats)]
        return pairs + [(w_down.at[cols, :], down.at[slot, j])]

    def own_copies(j):
        return [pltpu.make_async_copy(s, d, w_l.at[j, i]) for i, (s, d) in enumerate(weight_parts(j, yl))]

    def weight_sends(j):
        return [remote(s, d, w_s.at[j, i], w_r.at[j, i], mate) for i, (s, d) in enumerate(weight_parts(j, yl))]

    def weight_recvs(j):
        return [
            remote(d, d, w_s.at[j, i], w_r.at[j, i], mate)
            for i, (s, d) in enumerate(weight_parts(j, 1 - yl))
        ]

    for j in range(blocks):
        for copy in own_copies(j):
            copy.start()

    values = tokens[...].astype(F32)
    inverse = lax.rsqrt(jnp.mean(values * values, axis=1, keepdims=True) + 1e-05)
    both[...] = jnp.zeros_like(both)
    both[0:ROWS, :] = (values * inverse).astype(BF16).astype(F32)
    both[8 : 8 + ROWS, :] = grads[...].astype(F32)
    for q in range(8):
        parcels[q] = both[:, q * SLICE : (q + 1) * SLICE].astype(BF16)
    landed[me] = parcels[x * 2 + c]

    pl.semaphore_wait(barrier, PEERS - 1 + 3)

    def parcel(k):
        to = (me + k) % PEERS
        return remote(
            parcels.at[(to // 4) * 2 + to % 2], landed.at[me], a2a_s.at[k], a2a_r.at[k], peer(to)
        )

    def parcel_in(k):
        src = (me + PEERS - k) % PEERS
        return remote(landed.at[src], landed.at[src], a2a_s.at[k], a2a_r.at[k], peer(src))

    def start_parcel(k, carry):
        parcel(k).start()
        return carry

    def wait_parcel(k, carry):
        parcel_in(k).wait_recv()
        return carry

    lax.fori_loop(1, PEERS, start_parcel, 0)
    for copy in weight_sends(0):
        copy.start()
    lax.fori_loop(1, PEERS, wait_parcel, 0)

    col = lax.broadcasted_iota(jnp.int32, (2 * BLOCK, PEERS * 16), 1)
    row = lax.broadcasted_iota(jnp.int32, (2 * BLOCK, PEERS * 16), 0)
    source, place = col >> 4, col & 15
    kind, token = place >> 3, place & 7
    pick = (row == kind * BLOCK + source * ROWS + token) & (token < ROWS)
    packed = jnp.dot(
        jnp.where(pick, 1.0, 0.0).astype(BF16),
        landed[...].reshape(PEERS * 16, SLICE),
        preferred_element_type=F32,
    ).astype(BF16)
    tok[0, c, 0, 0] = packed[:BLOCK]
    tok[0, c, 1, 0] = packed[BLOCK:]

    def z_send(s, way, kind):
        src = tok.at[s, c, kind, way]
        if isinstance(s, int):
            src = tok.at[0, c, kind, 0]
        return remote(
            src,
            tok.at[s + 1, c, kind, way],
            z_s.at[s, way, kind],
            z_r.at[s + 1, way, kind],
            (above, below)[way],
        )

    def z_last(way):
        return remote(
            tok.at[PAIRS - 1, c, way, way],
            tok.at[0, c, way, 1],
            z_s.at[PAIRS - 1, way, way],
            z_r.at[0, 1, way],
            (above, below)[way],
        )

    def z_in(s, way, kind):
        return remote(tok.at[s, c, kind, way], tok.at[s, c, kind, way], z_s.at[s, way, kind], z_r.at[s, way, kind], above)

    def c_send(s, way, kind):
        piece = tok.at[s, c, kind, way]
        return remote(piece, piece, c_s.at[s, way, kind], c_r.at[s, way, kind], other)

    def c_in(s, way, kind):
        piece = tok.at[s, 1 - c, kind, way]
        return remote(piece, piece, c_s.at[s, way, kind], c_r.at[s, way, kind], other)

    for kind in range(2):
        for way in range(2):
            z_send(0, way, kind).start()
    for kind in range(2):
        c_send(0, 0, kind).start()

    def tokens_of(u):
        s = u + 1

        @pl.when(s < PAIRS)
        def _():
            for kind in range(2):
                for way in range(2):
                    z_in(s, way, kind).wait_recv()

                    @pl.when(s < PAIRS - 1)
                    def _(way=way, kind=kind):
                        z_send(s, way, kind).start()

                    if way == kind:

                        @pl.when(s == PAIRS - 1)
                        def _(way=way):
                            z_last(way).start()

                    c_send(s, way, kind).start()
            for kind in range(2):
                for way in range(2):
                    c_in(s, way, kind).wait_recv()

        @pl.when(s == PAIRS)
        def _():
            for kind in range(2):
                z_in(0, 1, kind).wait_recv()
                c_send(0, 1, kind).start()
            for kind in range(2):
                for way in range(2):
                    c_in(0, way, kind).wait_recv()

    bottom = STACK - TOP

    def x_copy(u, k, src, dst, to):
        return remote(src, dst, x_s.at[u, k], x_r.at[u, k], to)

    def scatter_sends(u):
        return [
            x_copy(u, 0, part.at[u, xo, pl.ds(0, TOP)], via_left.at[u], right),
            x_copy(u, 1, part.at[u, xo, pl.ds(TOP, bottom)], via_right.at[u], left),
            x_copy(u, 2, part.at[u, xr, pl.ds(TOP, bottom)], from_left.at[u, pl.ds(TOP, bottom)], right),
            x_copy(u, 3, part.at[u, xl, pl.ds(0, TOP)], from_right.at[u, pl.ds(0, TOP)], left),
        ]

    def mixed_sends(u):
        return [
            x_copy(u, 4, via_left.at[u], from_left.at[u, pl.ds(0, TOP)], right),
            x_copy(u, 5, via_right.at[u], from_right.at[u, pl.ds(TOP, bottom)], left),
        ]

    def tq_sends(u):
        return [
            x_copy(u, 6, tq.at[u, :, x], tq.at[u, :, x], right),
            x_copy(u, 7, tq.at[u, :, x], tq.at[u, :, x], left),
        ]

    def tq_ins(u):
        return [
            x_copy(u, 6, tq.at[u, :, xl], tq.at[u, :, xl], right),
            x_copy(u, 7, tq.at[u, :, xr], tq.at[u, :, xr], left),
        ]

    def tq_forwards(u):
        return [
            x_copy(u, 8, tq.at[u, 0, xl], tq.at[u, 0, xl], right),
            x_copy(u, 9, tq.at[u, 1, xr], tq.at[u, 1, xr], left),
        ]

    def tq_forward_ins(u):
        return [
            x_copy(u, 8, tq.at[u, 0, xo], tq.at[u, 0, xo], right),
            x_copy(u, 9, tq.at[u, 1, xo], tq.at[u, 1, xo], left),
        ]

    def products(u):
        j, i = u // PAIRS, u % PAIRS
        s = (i + 1) % PAIRS
        gates = jnp.zeros((UNIT, 4 * HB), F32)
        dhid = jnp.zeros((UNIT, HB), F32)
        for h in range(2):
            a = tok[s, h, 0].reshape(UNIT, SLICE)
            g = tok[s, h, 1].reshape(UNIT, SLICE)
            gates = gates + jnp.dot(a, wide[h, j], preferred_element_type=F32)
            dhid = dhid + lax.dot_general(g, down[h, j], (((1,), (1,)), ((), ())), preferred_element_type=F32)
        for q in range(NX):
            rows = slice(q * SHARE, (q + 1) * SHARE)
            for m in range(4):
                part[u, q, m * SHARE : (m + 1) * SHARE, :] = gates[rows, m * HB : (m + 1) * HB].astype(BF16)
            part[u, q, 4 * SHARE :, :] = (dhid[rows] * scale).astype(BF16)
        for copy in scatter_sends(u):
            copy.start()

    def mix(u):
        first, second = scatter_sends(u)[:2]
        first.wait_recv()
        via_left[u] = (via_left[u].astype(F32) + part[u, xr, :TOP].astype(F32)).astype(BF16)
        mixed_sends(u)[0].start()
        second.wait_recv()
        via_right[u] = (via_right[u].astype(F32) + part[u, xl, TOP:].astype(F32)).astype(BF16)
        mixed_sends(u)[1].start()

    def hidden(u):
        for copy in scatter_sends(u)[2:] + mixed_sends(u):
            copy.wait_recv()
        stack = part[u, x].astype(F32) + from_left[u].astype(F32) + from_right[u].astype(F32)
        gate, up, tgate, tup, dhid = (stack[m * SHARE : (m + 1) * SHARE] for m in range(5))
        sig = jax.nn.sigmoid(gate)
        first = sig * (1.0 + gate * (1.0 - sig))
        second = sig * (1.0 - sig) * (2.0 + gate * (1.0 - 2.0 * sig))
        tq[u, 0, x] = (dhid * (tup * first + up * second * tgate)).astype(BF16)
        tq[u, 1, x] = (dhid * first * tgate).astype(BF16)
        for copy in tq_sends(u):
            copy.start()

    def pass_on(u):
        for arrival, forward in zip(tq_ins(u), tq_forwards(u)):
            arrival.wait_recv()
            forward.start()

    def out_send(j):
        return remote(half_out.at[j], half_in.at[j], o_s.at[j], o_r.at[j], mate)

    def finish(u):
        j, i = u // PAIRS, u % PAIRS
        s = (i + 1) % PAIRS
        for copy in tq_forward_ins(u):
            copy.wait_recv()
        t = jnp.concatenate([tq[u, 0].reshape(UNIT, HB), tq[u, 1].reshape(UNIT, HB)], axis=1)
        for h in range(2):
            a = tok[s, h, 0].reshape(UNIT, SLICE)
            term = lax.dot_general(a, t, (((0,), (0,)), ((), ())), preferred_element_type=F32)

            @pl.when(i == 0)
            def _(h=h, term=term):
                total[j, h] = term

            @pl.when(i > 0)
            def _(h=h, term=term):
                total[j, h] += term

        @pl.when(i == PAIRS - 1)
        def _():
            half_out[j] = total[j, 1 - yl].astype(BF16)
            out_send(j).start()

        for copy in scatter_sends(u) + mixed_sends(u) + tq_sends(u) + tq_forwards(u):
            copy.wait_send()

    def step(n, carry):
        @pl.when(n < PAIRS)
        def _():
            tokens_of(n)

        for j in range(blocks):

            @pl.when(n == j * PAIRS)
            def _(j=j):
                for copy in own_copies(j):
                    copy.wait()
                for copy in weight_recvs(j):
                    copy.wait_recv()
                if j + 1 < blocks:
                    for copy in weight_sends(j + 1):
                        copy.start()

        for lag, stage in enumerate((products, mix, hidden, pass_on, finish)):

            @pl.when((n >= lag) & (n < units + lag))
            def _(lag=lag, stage=stage):
                stage(n - lag)

        return carry

    lax.fori_loop(0, units + LAG, step, 0)

    for j in range(blocks):
        out_send(j).wait_recv()
        mine = total[j, yl] + half_in[j].astype(F32)
        out_gate[:, j * HB : (j + 1) * HB] = mine[:, :HB]
        out_up[:, j * HB : (j + 1) * HB] = mine[:, HB:]

    def sent_parcel(k, carry):
        parcel(k).wait_send()
        return carry

    lax.fori_loop(1, PEERS, sent_parcel, 0)

    def sent_pieces(s, carry):
        for kind in range(2):
            for way in range(2):

                @pl.when(s < PAIRS - 1)
                def _(way=way, kind=kind):
                    z_send(s, way, kind).wait_send()

                c_send(s, way, kind).wait_send()
        return carry

    lax.fori_loop(0, PAIRS, sent_pieces, 0)
    for way in range(2):
        z_last(way).wait_send()
    for j in range(blocks):
        for copy in weight_sends(j):
            copy.wait_send()
        out_send(j).wait_send()


def per_device(tokens, w_gate, w_up, probe_gate, probe_up, w_down, out_grad):
    width = w_gate.shape[1]
    blocks = width // HB
    units = blocks * PAIRS
    everywhere = lax.axis_size("dp") * lax.axis_size("fsdp")
    scale = 1.0 / float(tokens.shape[0] * everywhere) ** 0.5
    dma = pltpu.SemaphoreType.DMA
    vmem, any_ = pl.BlockSpec(memory_space=pltpu.VMEM), pl.BlockSpec(memory_space=pl.ANY)
    return pl.pallas_call(
        functools.partial(kernel, blocks, scale),
        out_shape=(jax.ShapeDtypeStruct((SLICE, width), F32),) * 2,
        in_specs=[vmem] + [any_] * 5 + [vmem],
        out_specs=(vmem, vmem),
        scratch_shapes=[
            pltpu.VMEM((16, 8 * SLICE), F32),
            pltpu.VMEM((8, 16, SLICE), BF16),
            pltpu.VMEM((PEERS, 16, SLICE), BF16),
            pltpu.VMEM((PAIRS, 2, 2, 2, BLOCK, SLICE), BF16),
            pltpu.VMEM((2, blocks, SLICE, 4 * HB), BF16),
            pltpu.VMEM((2, blocks, HB, SLICE), BF16),
            pltpu.VMEM((units, NX, STACK, HB), BF16),
            pltpu.VMEM((units, TOP, HB), BF16),
            pltpu.VMEM((units, STACK - TOP, HB), BF16),
            pltpu.VMEM((units, STACK, HB), BF16),
            pltpu.VMEM((units, STACK, HB), BF16),
            pltpu.VMEM((units, 2, NX, SHARE, HB), BF16),
            pltpu.VMEM((blocks, 2, SLICE, 2 * HB), F32),
            pltpu.VMEM((blocks, SLICE, 2 * HB), BF16),
            pltpu.VMEM((blocks, SLICE, 2 * HB), BF16),
            dma((PEERS,)),
            dma((PEERS,)),
            dma((PAIRS, 2, 2)),
            dma((PAIRS, 2, 2)),
            dma((PAIRS, 2, 2)),
            dma((PAIRS, 2, 2)),
            dma((blocks, 5)),
            dma((blocks, 5)),
            dma((blocks, 5)),
            dma((units, 10)),
            dma((units, 10)),
            dma((blocks,)),
            dma((blocks,)),
        ],
        compiler_params=pltpu.CompilerParams(
            collective_id=0, has_side_effects=True, vmem_limit_bytes=48 * 1024 * 1024
        ),
    )(tokens, w_gate, w_up, probe_gate, probe_up, w_down, out_grad)


def solution(mesh):
    placed = (
        P(("dp", "fsdp"), None),
        P("dp", "fsdp"),
        P("dp", "fsdp"),
        P("dp", "fsdp"),
        P("dp", "fsdp"),
        P("fsdp", "dp"),
        P(("dp", "fsdp"), None),
    )
    return jax.shard_map(
        per_device,
        mesh=mesh,
        in_specs=placed,
        out_specs=(P("dp", "fsdp"), P("dp", "fsdp")),
        check_vma=False,
    )
```

```python
import functools

import jax
import jax.numpy as jnp
from jax import lax
from jax.experimental import pallas as pl
from jax.experimental.pallas import tpu as pltpu
from jax.sharding import PartitionSpec as P

MESH = pl.DeviceIdType.MESH
F32, BF16 = jnp.float32, jnp.bfloat16

NX, NY, NZ, NC = 4, 2, 16, 2
PEERS = NX * NY * NC
ROWS = 6
BLOCK = PEERS * ROWS
SLICE = 512
PAIRS = NZ // 2
UNIT = 2 * BLOCK
SHARE = UNIT // NX
STACK = 5 * SHARE
TOP = 128
HB = 128
LAG = 4
DIRECT = 2
SLOTS = 8
CUTS = 2
PIECE = BLOCK // CUTS
AHEAD = 4
TICKS = 2 * CUTS * PAIRS


def kernel(
    blocks,
    scale,
    tokens,
    w_gate,
    w_up,
    probe_gate,
    probe_up,
    w_down,
    grads,
    own_gate,
    own_up,
    in_gate,
    in_up,
    both,
    parcels,
    landed,
    tok,
    wide,
    down,
    part,
    via,
    from_left,
    from_right,
    tq,
    total,
    half_out,
    a2a_s,
    a2a_r,
    z_s,
    z_last_s,
    z_r,
    c_s,
    c_r,
    w_l,
    w_s,
    w_r,
    x_s,
    x_r,
    o_s,
    o_r,
    o_l,
):
    dp, fsdp = lax.axis_index("dp"), lax.axis_index("fsdp")
    x, yl = dp // 2, dp % 2
    yh, z, c = fsdp // 32, (fsdp // 2) % NZ, fsdp % 2
    units = blocks * PAIRS

    def device(x_, yl_, yh_, z_, c_):
        return (x_ * 2 + yl_, yh_ * 32 + z_ * 2 + c_)

    xr, xl, xo = (x + 1) % NX, (x + 3) % NX, (x + 2) % NX
    zr, zl = (z + 1) % NZ, (z + NZ - 1) % NZ
    right, left = device(xr, yl, yh, z, c), device(xl, yl, yh, z, c)
    above, below = device(x, yl, yh, zr, c), device(x, yl, yh, zl, c)
    other = device(x, yl, yh, z, 1 - c)
    mate = device(x, 1 - yl, yh, z, c)
    me = x * 4 + yh * 2 + c

    def peer(index):
        return device(index // 4, yl, (index // 2) % 2, z, index % 2)

    def remote(src, dst, send, recv, to):
        return pltpu.make_async_remote_copy(
            src_ref=src, dst_ref=dst, send_sem=send, recv_sem=recv, device_id=to, device_id_type=MESH
        )

    barrier = pltpu.get_barrier_semaphore()

    def greet(k, carry):
        pl.semaphore_signal(barrier, inc=1, device_id=peer((me + k) % PEERS), device_id_type=MESH)
        return carry

    lax.fori_loop(1, PEERS, greet, 0)
    for to in (above, below, mate):
        pl.semaphore_signal(barrier, inc=1, device_id=to, device_id_type=MESH)

    mats = (w_gate, w_up, probe_gate, probe_up)

    def weight_parts(j, slot):
        cols = pl.ds(j * HB, HB)
        pairs = [(m.at[:, cols], wide.at[slot, j, :, pl.ds(i * HB, HB)]) for i, m in enumerate(mats)]
        return pairs + [(w_down.at[cols, :], down.at[slot, j])]

    def own_copies(j):
        return [
            pltpu.make_async_copy(s, d, w_l.at[j, i // 4]) for i, (s, d) in enumerate(weight_parts(j, yl))
        ]

    def weight_sends(j):
        return [
            remote(s, d, w_s.at[j, i // 4], w_r.at[j, i // 4], mate)
            for i, (s, d) in enumerate(weight_parts(j, yl))
        ]

    def weights_whole(j, slot):
        return [
            remote(ref.at[slot, j], ref.at[slot, j], w_s.at[j, i], w_r.at[j, i], mate)
            for i, ref in enumerate((wide, down))
        ]

    def own_whole(j):
        return [
            pltpu.make_async_copy(ref.at[yl, j], ref.at[yl, j], w_l.at[j, i])
            for i, ref in enumerate((wide, down))
        ]

    for j in range(blocks):
        for copy in own_copies(j):
            copy.start()

    values = tokens[...].astype(F32)
    inverse = lax.rsqrt(jnp.mean(values * values, axis=1, keepdims=True) + 1e-05)
    both[...] = jnp.zeros_like(both)
    both[0:ROWS, :] = (values * inverse).astype(BF16).astype(F32)
    both[8 : 8 + ROWS, :] = grads[...].astype(F32)
    for q in range(8):
        parcels[q] = both[:, q * SLICE : (q + 1) * SLICE].astype(BF16)
    landed[me] = parcels[x * 2 + c]

    pl.semaphore_wait(barrier, PEERS - 1 + 3)

    def start_parcel(k, carry):
        to = (me + k) % PEERS
        remote(
            parcels.at[(to // 4) * 2 + to % 2], landed.at[me], a2a_s.at[0], a2a_r.at[0], peer(to)
        ).start()
        return carry

    lax.fori_loop(1, PEERS, start_parcel, 0)
    for copy in weight_sends(0):
        copy.start()
    parcels_whole = remote(
        landed.at[pl.ds(0, PEERS - 1)], landed.at[pl.ds(0, PEERS - 1)], a2a_s.at[0], a2a_r.at[0], other
    )
    parcels_whole.wait_recv()

    col = lax.broadcasted_iota(jnp.int32, (2 * BLOCK, PEERS * 16), 1)
    row = lax.broadcasted_iota(jnp.int32, (2 * BLOCK, PEERS * 16), 0)
    source, place = col >> 4, col & 15
    kind, token = place >> 3, place & 7
    pick = (row == kind * BLOCK + source * ROWS + token) & (token < ROWS)
    packed = jnp.dot(
        jnp.where(pick, 1.0, 0.0).astype(BF16),
        landed[...].reshape(PEERS * 16, SLICE),
        preferred_element_type=F32,
    ).astype(BF16)
    tok[0, c, 0, 0] = packed[:BLOCK].reshape(CUTS, PIECE, SLICE)
    tok[0, c, 1, 0] = packed[BLOCK:].reshape(CUTS, PIECE, SLICE)

    def z_send(s, way, kind, cut):
        src = tok.at[s, c, kind, 0 if isinstance(s, int) else way, cut]
        return remote(
            src, tok.at[s + 1, c, kind, way, cut], z_s.at[0], z_r.at[s + 1, way, kind, cut], (above, below)[way]
        )

    def z_last(way, cut):
        to = device(x, yl, yh, (z + 1 + way * (NZ - 2)) % NZ, c)
        src, dst = tok.at[PAIRS - 1, c, way, way, cut], tok.at[0, c, way, 1, cut]
        return remote(src, dst, z_last_s.at[0], z_r.at[0, 1, way, cut], to)

    def z_in(s, way, kind, cut):
        piece = tok.at[s, c, kind, way, cut]
        return remote(piece, piece, z_s.at[0], z_r.at[s, way, kind, cut], above)

    def c_send(s, way, kind):
        piece = tok.at[s, c, kind, way]
        return remote(piece, piece, c_s.at[0], c_r.at[s], other)

    def c_in(s):
        return remote(tok.at[s, 1 - c], tok.at[s, 1 - c], c_s.at[0], c_r.at[s], other)

    for kind in range(2):
        for cut in range(CUTS):
            for way in range(2):
                z_send(0, way, kind, cut).start()
    for kind in range(2):
        c_send(0, 0, kind).start()

    def tick(k, carry=None):
        s, kind, cut = k // (2 * CUTS) + 1, (k // CUTS) % 2, k % CUTS

        @pl.when(s < PAIRS)
        def _():
            for way in range(2):
                z_in(s, way, kind, cut).wait_recv()

                @pl.when(s < PAIRS - 1)
                def _(way=way):
                    z_send(s, way, kind, cut).start()

            @pl.when(s == PAIRS - 1)
            def _():
                z_last(kind, cut).start()

            @pl.when(cut == CUTS - 1)
            def _():
                for way in range(2):
                    c_send(s, way, kind).start()

        @pl.when(s == PAIRS)
        def _():
            z_in(0, 1, kind, cut).wait_recv()

            @pl.when(cut == CUTS - 1)
            def _():
                c_send(0, 1, kind).start()

        return carry

    lax.fori_loop(0, AHEAD, tick, 0)

    def place(n):
        quarter = n // (PAIRS // 2)
        mixed = ((quarter + 1) // 2) % 2
        last = quarter // 3
        j = mixed * (1 - n % 2) + last
        i = (1 - mixed - last) * n + mixed * (n // 2 - 2 + (n % 2) * 4) + last * (n - PAIRS)
        return j, i

    bottom = STACK - TOP

    F_LEFT, F_RIGHT, LEFT, RIGHT, T_LEFT, T_RIGHT, T_FAR = range(7)
    SCATTER, MIXED, TQ, PASSED = range(4)
    far = device(xo, yl, yh, z, c)

    def x_copy(u, send, recv, src, dst, to):
        slot = u % SLOTS
        return remote(src, dst, x_s.at[slot, send], x_r.at[slot, recv], to)

    def x_start(u, send, *copies):
        for recv, src, dst, to in copies:
            x_copy(u, send, recv, src, dst, to).start()

    def x_wait(u, recv, ref):
        x_copy(u, 0, recv, ref, ref, far).wait_recv()

    def x_sent(u, send, ref):
        x_copy(u, send, 0, ref, ref, far).wait_send()

    top, low = pl.ds(0, TOP), pl.ds(TOP, bottom)

    def ring(u):
        return u < units - DIRECT

    def products(u):
        j, i = place(u)
        s = (i + 1) % PAIRS
        gates = jnp.zeros((UNIT, 4 * HB), F32)
        dhid = jnp.zeros((UNIT, HB), F32)
        for h in range(2):
            a = tok[s, h, 0].reshape(UNIT, SLICE)
            g = tok[s, h, 1].reshape(UNIT, SLICE)
            gates = gates + jnp.dot(a, wide[h, j], preferred_element_type=F32)
            dhid = dhid + lax.dot_general(g, down[h, j], (((1,), (1,)), ((), ())), preferred_element_type=F32)
        for q in range(NX):
            rows = slice(q * SHARE, (q + 1) * SHARE)
            for m in range(4):
                part[u, q, m * SHARE : (m + 1) * SHARE, :] = gates[rows, m * HB : (m + 1) * HB].astype(BF16)
            part[u, q, 4 * SHARE :, :] = (dhid[rows] * scale).astype(BF16)

        @pl.when(ring(u))
        def _():
            x_start(
                u,
                SCATTER,
                (F_LEFT, part.at[u, xo, top], via.at[u, top], right),
                (F_RIGHT, part.at[u, xo, low], via.at[u, low], left),
                (LEFT, part.at[u, xr, low], from_left.at[u, low], right),
                (RIGHT, part.at[u, xl, top], from_right.at[u, top], left),
            )

        @pl.when(u >= units - DIRECT)
        def _():
            x_start(
                u,
                SCATTER,
                (F_LEFT, part.at[u, xo], via.at[u], far),
                (LEFT, part.at[u, xr], from_left.at[u], right),
                (RIGHT, part.at[u, xl], from_right.at[u], left),
            )

    def mix(u):
        @pl.when(ring(u))
        def _():
            x_wait(u, F_LEFT, via.at[u, top])
            via[u, :TOP] = (via[u, :TOP].astype(F32) + part[u, xr, :TOP].astype(F32)).astype(BF16)
            x_start(u, MIXED, (LEFT, via.at[u, top], from_left.at[u, top], right))
            x_wait(u, F_RIGHT, via.at[u, low])
            via[u, TOP:] = (via[u, TOP:].astype(F32) + part[u, xl, TOP:].astype(F32)).astype(BF16)
            x_start(u, MIXED, (RIGHT, via.at[u, low], from_right.at[u, low], left))

    def activate(u, stack):
        gate, up, tgate, tup, dhid = (stack[m * SHARE : (m + 1) * SHARE] for m in range(5))
        sig = jax.nn.sigmoid(gate)
        first = sig * (1.0 + gate * (1.0 - sig))
        second = sig * (1.0 - sig) * (2.0 + gate * (1.0 - 2.0 * sig))
        tq[u, 0, x] = (dhid * (tup * first + up * second * tgate)).astype(BF16)
        tq[u, 1, x] = (dhid * first * tgate).astype(BF16)
        x_start(
            u,
            TQ,
            (T_LEFT, tq.at[u, :, x], tq.at[u, :, x], right),
            (T_RIGHT, tq.at[u, :, x], tq.at[u, :, x], left),
        )

    def hidden(u):
        x_wait(u, LEFT, from_left.at[u])
        x_wait(u, RIGHT, from_right.at[u])

        @pl.when(ring(u))
        def _():
            activate(u, part[u, x].astype(F32) + from_left[u].astype(F32) + from_right[u].astype(F32))

        @pl.when(u >= units - DIRECT)
        def _():
            x_wait(u, F_LEFT, via.at[u])
            near = part[u, x].astype(F32) + from_left[u].astype(F32)
            activate(u, near + from_right[u].astype(F32) + via[u].astype(F32))
            x_start(u, TQ, (T_FAR, tq.at[u, :, x], tq.at[u, :, x], far))

    def pass_on(u):
        @pl.when(ring(u))
        def _():
            x_wait(u, T_LEFT, tq.at[u, :, xl])
            x_start(u, PASSED, (T_FAR, tq.at[u, 0, xl], tq.at[u, 0, xl], right))
            x_wait(u, T_RIGHT, tq.at[u, :, xr])
            x_start(u, PASSED, (T_FAR, tq.at[u, 1, xr], tq.at[u, 1, xr], left))

    def out_sends(j):
        cols = pl.ds(j * HB, HB)
        return [
            remote(half_out.at[j, g], ref.at[:, cols], o_s.at[j, g], o_r.at[j, g], mate)
            for g, ref in enumerate((in_gate, in_up))
        ]

    def out_copies(j):
        cols = pl.ds(j * HB, HB)
        return [
            pltpu.make_async_copy(total.at[j, yl, :, pl.ds(g * HB, HB)], ref.at[:, cols], o_l.at[j, g])
            for g, ref in enumerate((own_gate, own_up))
        ]

    def finish(u):
        j, i = place(u)
        s = (i + 1) % PAIRS

        @pl.when(u >= units - DIRECT)
        def _():
            x_wait(u, T_LEFT, tq.at[u, :, xl])
            x_wait(u, T_RIGHT, tq.at[u, :, xr])

        x_wait(u, T_FAR, tq.at[u, :, xo])
        t = jnp.concatenate([tq[u, 0].reshape(UNIT, HB), tq[u, 1].reshape(UNIT, HB)], axis=1)
        for h in (1 - yl, yl):
            a = tok[s, h, 0].reshape(UNIT, SLICE)
            term = lax.dot_general(a, t, (((0,), (0,)), ((), ())), preferred_element_type=F32)

            @pl.when(i == 0)
            def _(h=h, term=term):
                total[j, h] = term

            @pl.when(i > 0)
            def _(h=h, term=term):
                total[j, h] += term

            if h is not yl:
                for jj in range(blocks):

                    @pl.when((i == PAIRS - 1) & (j == jj))
                    def _(jj=jj):
                        for g, copy in enumerate(out_sends(jj)):
                            half_out[jj, g] = total[jj, 1 - yl, :, g * HB : (g + 1) * HB].astype(BF16)
                            copy.start()

        for jj in range(blocks):

            @pl.when((i == PAIRS - 1) & (j == jj))
            def _(jj=jj):
                for copy in out_copies(jj):
                    copy.start()

        @pl.when(ring(u))
        def _():
            x_sent(u, SCATTER, part.at[u, pl.ds(0, 2)])
            x_sent(u, MIXED, part.at[u, 0])
            x_sent(u, TQ, tq.at[u, :, pl.ds(0, 2)])
            x_sent(u, PASSED, tq.at[u, :, 0])

        @pl.when(u >= units - DIRECT)
        def _():
            x_sent(u, SCATTER, part.at[u, pl.ds(0, 3)])
            x_sent(u, TQ, tq.at[u, :, pl.ds(0, 3)])

    def step(n, carry):
        j, i = place(n)

        def ticks(lag):
            if lag in (0, 1, 2, 4):

                @pl.when(n < PAIRS // 2)
                def _():
                    tick(AHEAD + 4 * n + min(lag, 3))

            if lag in (0, 2):
                k = AHEAD + 4 * (PAIRS // 2) + 2 * (n - PAIRS // 2) + lag // 2

                @pl.when((n >= PAIRS // 2) & (k < TICKS))
                def _():
                    tick(k)

        ticks(0)

        @pl.when((n < 3 * PAIRS // 2) & (j == 0))
        def _():
            c_in((i + 1) % PAIRS).wait_recv()

        for jj in range(blocks):

            @pl.when(n == jj * (PAIRS // 2))
            def _(jj=jj):
                for copy in own_whole(jj):
                    copy.wait()
                for copy in weights_whole(jj, 1 - yl):
                    copy.wait_recv()
                if jj + 1 < blocks:
                    for copy in weight_sends(jj + 1):
                        copy.start()

        for lag, stage in enumerate((products, mix, hidden, pass_on, finish)):
            if lag:
                ticks(lag)

            @pl.when((n >= lag) & (n < units + lag))
            def _(lag=lag, stage=stage):
                stage(n - lag)

        return carry

    lax.fori_loop(0, units + LAG, step, 0)

    parcels_whole.wait_send()
    first_steps, half = tok.at[pl.ds(0, PAIRS - 1), c], tok.at[:, c]
    remote(first_steps, first_steps, z_s.at[0], z_r.at[0, 0, 0, 0], above).wait_send()
    remote(tok.at[0, c, 0], tok.at[0, c, 0], z_last_s.at[0], z_r.at[0, 0, 0, 0], above).wait_send()
    remote(half, half, c_s.at[0], c_r.at[0], other).wait_send()
    for j in range(blocks):
        for copy in weights_whole(j, yl):
            copy.wait_send()
        for copy in out_copies(j):
            copy.wait()
    for j in range(blocks):
        for copy in out_sends(j):
            copy.wait()


def per_device(tokens, w_gate, w_up, probe_gate, probe_up, w_down, out_grad):
    width = w_gate.shape[1]
    blocks = width // HB
    units = blocks * PAIRS
    everywhere = lax.axis_size("dp") * lax.axis_size("fsdp")
    scale = 1.0 / float(tokens.shape[0] * everywhere) ** 0.5
    dma = pltpu.SemaphoreType.DMA
    vmem, any_ = pl.BlockSpec(memory_space=pltpu.VMEM), pl.BlockSpec(memory_space=pl.ANY)
    own_gate, own_up, in_gate, in_up = pl.pallas_call(
        functools.partial(kernel, blocks, scale),
        out_shape=(jax.ShapeDtypeStruct((SLICE, width), F32),) * 2
        + (jax.ShapeDtypeStruct((SLICE, width), BF16),) * 2,
        in_specs=[vmem] + [any_] * 5 + [vmem],
        out_specs=(any_,) * 4,
        scratch_shapes=[
            pltpu.VMEM((16, 8 * SLICE), F32),
            pltpu.VMEM((8, 16, SLICE), BF16),
            pltpu.VMEM((PEERS, 16, SLICE), BF16),
            pltpu.VMEM((PAIRS, 2, 2, 2, CUTS, PIECE, SLICE), BF16),
            pltpu.VMEM((2, blocks, SLICE, 4 * HB), BF16),
            pltpu.VMEM((2, blocks, HB, SLICE), BF16),
            pltpu.VMEM((units, NX, STACK, HB), BF16),
            pltpu.VMEM((units, STACK, HB), BF16),
            pltpu.VMEM((units, STACK, HB), BF16),
            pltpu.VMEM((units, STACK, HB), BF16),
            pltpu.VMEM((units, 2, NX, SHARE, HB), BF16),
            pltpu.VMEM((blocks, 2, SLICE, 2 * HB), F32),
            pltpu.VMEM((blocks, 2, SLICE, HB), BF16),
            dma((1,)),
            dma((1,)),
            dma((1,)),
            dma((1,)),
            dma((PAIRS, 2, 2, CUTS)),
            dma((1,)),
            dma((PAIRS,)),
            dma((blocks, 2)),
            dma((blocks, 2)),
            dma((blocks, 2)),
            dma((SLOTS, 4)),
            dma((SLOTS, 7)),
            dma((blocks, 2)),
            dma((blocks, 2)),
            dma((blocks, 2)),
        ],
        compiler_params=pltpu.CompilerParams(
            collective_id=0, has_side_effects=True, vmem_limit_bytes=62 * 1024 * 1024
        ),
    )(tokens, w_gate, w_up, probe_gate, probe_up, w_down, out_grad)
    return own_gate + in_gate.astype(F32), own_up + in_up.astype(F32)


def solution(mesh):
    placed = (
        P(("dp", "fsdp"), None),
        P("dp", "fsdp"),
        P("dp", "fsdp"),
        P("dp", "fsdp"),
        P("dp", "fsdp"),
        P("fsdp", "dp"),
        P(("dp", "fsdp"), None),
    )
    return jax.shard_map(
        per_device,
        mesh=mesh,
        in_specs=placed,
        out_specs=(P("dp", "fsdp"), P("dp", "fsdp")),
        check_vma=False,
    )
```

```python
import functools

import jax
import jax.numpy as jnp
from jax import lax
from jax.experimental import pallas as pl
from jax.experimental.pallas import tpu as pltpu
from jax.sharding import PartitionSpec as P

MESH = pl.DeviceIdType.MESH
F32, BF16 = jnp.float32, jnp.bfloat16

NX, NY, NZ, NC = 4, 2, 16, 2
PEERS = NX * NY * NC
ROWS = 6
BLOCK = PEERS * ROWS
SLICE = 512
PAIRS = NZ // 2
UNIT = 2 * BLOCK
SHARE = UNIT // NX
STACK = 5 * SHARE
TOP = 128
HB = 128
LAGS = (0, 2, 4, 6, 8)
DIRECT = 0
SLOTS = 10
CUTS = 2
PIECE = BLOCK // CUTS
AHEAD = 4
TICKS = 2 * CUTS * PAIRS


def kernel(
    blocks,
    scale,
    tokens,
    w_gate,
    w_up,
    probe_gate,
    probe_up,
    w_down,
    grads,
    own_gate,
    own_up,
    in_gate,
    in_up,
    both,
    parcels,
    landed,
    tok,
    wide,
    down,
    part,
    via,
    from_left,
    from_right,
    tq,
    total,
    half_out,
    a2a_s,
    a2a_r,
    z_s,
    z_last_s,
    z_r,
    c_s,
    c_r,
    w_l,
    w_s,
    w_r,
    x_s,
    x_r,
    o_s,
    o_r,
    o_l,
):
    dp, fsdp = lax.axis_index("dp"), lax.axis_index("fsdp")
    x, yl = dp // 2, dp % 2
    yh, z, c = fsdp // 32, (fsdp // 2) % NZ, fsdp % 2
    units = blocks * PAIRS

    def device(x_, yl_, yh_, z_, c_):
        return (x_ * 2 + yl_, yh_ * 32 + z_ * 2 + c_)

    xr, xl, xo = (x + 1) % NX, (x + 3) % NX, (x + 2) % NX
    zr, zl = (z + 1) % NZ, (z + NZ - 1) % NZ
    right, left = device(xr, yl, yh, z, c), device(xl, yl, yh, z, c)
    above, below = device(x, yl, yh, zr, c), device(x, yl, yh, zl, c)
    other = device(x, yl, yh, z, 1 - c)
    mate = device(x, 1 - yl, yh, z, c)
    me = x * 4 + yh * 2 + c

    def peer(index):
        return device(index // 4, yl, (index // 2) % 2, z, index % 2)

    def remote(src, dst, send, recv, to):
        return pltpu.make_async_remote_copy(
            src_ref=src, dst_ref=dst, send_sem=send, recv_sem=recv, device_id=to, device_id_type=MESH
        )

    barrier = pltpu.get_barrier_semaphore()

    def greet(k, carry):
        pl.semaphore_signal(barrier, inc=1, device_id=peer((me + k) % PEERS), device_id_type=MESH)
        return carry

    lax.fori_loop(1, PEERS, greet, 0)
    for to in (above, below, mate):
        pl.semaphore_signal(barrier, inc=1, device_id=to, device_id_type=MESH)

    mats = (w_gate, w_up, probe_gate, probe_up)

    def weight_parts(j, slot):
        cols = pl.ds(j * HB, HB)
        pairs = [(m.at[:, cols], wide.at[slot, j, :, pl.ds(i * HB, HB)]) for i, m in enumerate(mats)]
        return pairs + [(w_down.at[cols, :], down.at[slot, j])]

    def own_copies(j):
        return [
            pltpu.make_async_copy(s, d, w_l.at[j, i // 4]) for i, (s, d) in enumerate(weight_parts(j, yl))
        ]

    def weight_sends(j):
        return [
            remote(s, d, w_s.at[j, i // 4], w_r.at[j, i // 4], mate)
            for i, (s, d) in enumerate(weight_parts(j, yl))
        ]

    def weights_whole(j, slot):
        return [
            remote(ref.at[slot, j], ref.at[slot, j], w_s.at[j, i], w_r.at[j, i], mate)
            for i, ref in enumerate((wide, down))
        ]

    def own_whole(j):
        return [
            pltpu.make_async_copy(ref.at[yl, j], ref.at[yl, j], w_l.at[j, i])
            for i, ref in enumerate((wide, down))
        ]

    for j in range(blocks):
        for copy in own_copies(j):
            copy.start()

    values = tokens[...].astype(F32)
    inverse = lax.rsqrt(jnp.mean(values * values, axis=1, keepdims=True) + 1e-05)
    both[...] = jnp.zeros_like(both)
    both[0:ROWS, :] = (values * inverse).astype(BF16).astype(F32)
    both[8 : 8 + ROWS, :] = grads[...].astype(F32)
    for q in range(8):
        parcels[q] = both[:, q * SLICE : (q + 1) * SLICE].astype(BF16)
    landed[me] = parcels[x * 2 + c]

    pl.semaphore_wait(barrier, PEERS - 1 + 3)

    def start_parcel(k, carry):
        to = (me + k) % PEERS
        remote(
            parcels.at[(to // 4) * 2 + to % 2], landed.at[me], a2a_s.at[0], a2a_r.at[0], peer(to)
        ).start()
        return carry

    lax.fori_loop(1, PEERS, start_parcel, 0)
    for copy in weight_sends(0):
        copy.start()
    parcels_whole = remote(
        landed.at[pl.ds(0, PEERS - 1)], landed.at[pl.ds(0, PEERS - 1)], a2a_s.at[0], a2a_r.at[0], other
    )
    parcels_whole.wait_recv()

    col = lax.broadcasted_iota(jnp.int32, (2 * BLOCK, PEERS * 16), 1)
    row = lax.broadcasted_iota(jnp.int32, (2 * BLOCK, PEERS * 16), 0)
    source, place = col >> 4, col & 15
    kind, token = place >> 3, place & 7
    pick = (row == kind * BLOCK + source * ROWS + token) & (token < ROWS)
    packed = jnp.dot(
        jnp.where(pick, 1.0, 0.0).astype(BF16),
        landed[...].reshape(PEERS * 16, SLICE),
        preferred_element_type=F32,
    ).astype(BF16)
    tok[0, c, 0, 0] = packed[:BLOCK].reshape(CUTS, PIECE, SLICE)
    tok[0, c, 1, 0] = packed[BLOCK:].reshape(CUTS, PIECE, SLICE)

    def z_send(s, way, kind, cut):
        src = tok.at[s, c, kind, 0 if isinstance(s, int) else way, cut]
        return remote(
            src, tok.at[s + 1, c, kind, way, cut], z_s.at[0], z_r.at[s + 1, way, kind, cut], (above, below)[way]
        )

    def z_last(way, cut):
        to = device(x, yl, yh, (z + 1 + way * (NZ - 2)) % NZ, c)
        src, dst = tok.at[PAIRS - 1, c, way, way, cut], tok.at[0, c, way, 1, cut]
        return remote(src, dst, z_last_s.at[0], z_r.at[0, 1, way, cut], to)

    def z_in(s, way, kind, cut):
        piece = tok.at[s, c, kind, way, cut]
        return remote(piece, piece, z_s.at[0], z_r.at[s, way, kind, cut], above)

    def c_send(s, way, kind):
        piece = tok.at[s, c, kind, way]
        return remote(piece, piece, c_s.at[0], c_r.at[s], other)

    def c_in(s):
        return remote(tok.at[s, 1 - c], tok.at[s, 1 - c], c_s.at[0], c_r.at[s], other)

    for kind in range(2):
        for cut in range(CUTS):
            for way in range(2):
                z_send(0, way, kind, cut).start()
    for kind in range(2):
        c_send(0, 0, kind).start()

    def tick(k, carry=None):
        s, kind, cut = k // (2 * CUTS) + 1, (k // CUTS) % 2, k % CUTS

        @pl.when(s < PAIRS)
        def _():
            for way in range(2):
                z_in(s, way, kind, cut).wait_recv()

                @pl.when(s < PAIRS - 1)
                def _(way=way):
                    z_send(s, way, kind, cut).start()

            @pl.when(s == PAIRS - 1)
            def _():
                z_last(kind, cut).start()

            @pl.when(cut == CUTS - 1)
            def _():
                for way in range(2):
                    c_send(s, way, kind).start()

        @pl.when(s == PAIRS)
        def _():
            z_in(0, 1, kind, cut).wait_recv()

            @pl.when(cut == CUTS - 1)
            def _():
                c_send(0, 1, kind).start()

        return carry

    lax.fori_loop(0, AHEAD, tick, 0)

    def place(n):
        quarter = n // (PAIRS // 2)
        mixed = ((quarter + 1) // 2) % 2
        last = quarter // 3
        j = mixed * (1 - n % 2) + last
        i = (1 - mixed - last) * n + mixed * (n // 2 - 2 + (n % 2) * 4) + last * (n - PAIRS)
        return j, i

    bottom = STACK - TOP

    F_LEFT, F_RIGHT, LEFT, RIGHT, T_LEFT, T_RIGHT, T_FAR = range(7)
    SCATTER, MIXED, TQ, PASSED = range(4)
    far = device(xo, yl, yh, z, c)

    def x_copy(u, send, recv, src, dst, to):
        slot = u % SLOTS
        return remote(src, dst, x_s.at[slot, send], x_r.at[slot, recv], to)

    def x_start(u, send, *copies):
        for recv, src, dst, to in copies:
            x_copy(u, send, recv, src, dst, to).start()

    def x_wait(u, recv, ref):
        x_copy(u, 0, recv, ref, ref, far).wait_recv()

    def x_sent(u, send, ref):
        x_copy(u, send, 0, ref, ref, far).wait_send()

    top, low = pl.ds(0, TOP), pl.ds(TOP, bottom)

    def ring(u):
        return u < units - DIRECT

    def products(u):
        j, i = place(u)
        s = (i + 1) % PAIRS
        gates = jnp.zeros((UNIT, 4 * HB), F32)
        dhid = jnp.zeros((UNIT, HB), F32)
        for h in range(2):
            a = tok[s, h, 0].reshape(UNIT, SLICE)
            g = tok[s, h, 1].reshape(UNIT, SLICE)
            gates = gates + jnp.dot(a, wide[h, j], preferred_element_type=F32)
            dhid = dhid + lax.dot_general(g, down[h, j], (((1,), (1,)), ((), ())), preferred_element_type=F32)
        for q in range(NX):
            rows = slice(q * SHARE, (q + 1) * SHARE)
            for m in range(4):
                part[u, q, m * SHARE : (m + 1) * SHARE, :] = gates[rows, m * HB : (m + 1) * HB].astype(BF16)
            part[u, q, 4 * SHARE :, :] = (dhid[rows] * scale).astype(BF16)

        @pl.when(ring(u))
        def _():
            x_start(
                u,
                SCATTER,
                (F_LEFT, part.at[u, xo, top], via.at[u, top], right),
                (F_RIGHT, part.at[u, xo, low], via.at[u, low], left),
                (LEFT, part.at[u, xr, low], from_left.at[u, low], right),
                (RIGHT, part.at[u, xl, top], from_right.at[u, top], left),
            )

        @pl.when(u >= units - DIRECT)
        def _():
            x_start(
                u,
                SCATTER,
                (F_LEFT, part.at[u, xo], via.at[u], far),
                (LEFT, part.at[u, xr], from_left.at[u], right),
                (RIGHT, part.at[u, xl], from_right.at[u], left),
            )

    def mix(u):
        @pl.when(ring(u))
        def _():
            x_wait(u, F_LEFT, via.at[u, top])
            via[u, :TOP] = (via[u, :TOP].astype(F32) + part[u, xr, :TOP].astype(F32)).astype(BF16)
            x_start(u, MIXED, (LEFT, via.at[u, top], from_left.at[u, top], right))
            x_wait(u, F_RIGHT, via.at[u, low])
            via[u, TOP:] = (via[u, TOP:].astype(F32) + part[u, xl, TOP:].astype(F32)).astype(BF16)
            x_start(u, MIXED, (RIGHT, via.at[u, low], from_right.at[u, low], left))

    def activate(u, stack):
        gate, up, tgate, tup, dhid = (stack[m * SHARE : (m + 1) * SHARE] for m in range(5))
        sig = jax.nn.sigmoid(gate)
        first = sig * (1.0 + gate * (1.0 - sig))
        second = sig * (1.0 - sig) * (2.0 + gate * (1.0 - 2.0 * sig))
        tq[u, 0, x] = (dhid * (tup * first + up * second * tgate)).astype(BF16)
        tq[u, 1, x] = (dhid * first * tgate).astype(BF16)
        x_start(
            u,
            TQ,
            (T_LEFT, tq.at[u, :, x], tq.at[u, :, x], right),
            (T_RIGHT, tq.at[u, :, x], tq.at[u, :, x], left),
        )

    def hidden(u):
        x_wait(u, LEFT, from_left.at[u])
        x_wait(u, RIGHT, from_right.at[u])

        @pl.when(ring(u))
        def _():
            activate(u, part[u, x].astype(F32) + from_left[u].astype(F32) + from_right[u].astype(F32))

        @pl.when(u >= units - DIRECT)
        def _():
            x_wait(u, F_LEFT, via.at[u])
            near = part[u, x].astype(F32) + from_left[u].astype(F32)
            activate(u, near + from_right[u].astype(F32) + via[u].astype(F32))
            x_start(u, TQ, (T_FAR, tq.at[u, :, x], tq.at[u, :, x], far))

    def pass_on(u):
        @pl.when(ring(u))
        def _():
            x_wait(u, T_LEFT, tq.at[u, :, xl])
            x_start(u, PASSED, (T_FAR, tq.at[u, 0, xl], tq.at[u, 0, xl], right))
            x_wait(u, T_RIGHT, tq.at[u, :, xr])
            x_start(u, PASSED, (T_FAR, tq.at[u, 1, xr], tq.at[u, 1, xr], left))

    def out_sends(j):
        cols = pl.ds(j * HB, HB)
        return [
            remote(half_out.at[j, g], ref.at[:, cols], o_s.at[j, g], o_r.at[j, g], mate)
            for g, ref in enumerate((in_gate, in_up))
        ]

    def out_copies(j):
        cols = pl.ds(j * HB, HB)
        return [
            pltpu.make_async_copy(total.at[j, yl, :, pl.ds(g * HB, HB)], ref.at[:, cols], o_l.at[j, g])
            for g, ref in enumerate((own_gate, own_up))
        ]

    def finish(u):
        j, i = place(u)
        s = (i + 1) % PAIRS

        @pl.when(u >= units - DIRECT)
        def _():
            x_wait(u, T_LEFT, tq.at[u, :, xl])
            x_wait(u, T_RIGHT, tq.at[u, :, xr])

        x_wait(u, T_FAR, tq.at[u, :, xo])
        t = jnp.concatenate([tq[u, 0].reshape(UNIT, HB), tq[u, 1].reshape(UNIT, HB)], axis=1)
        for h in (1 - yl, yl):
            a = tok[s, h, 0].reshape(UNIT, SLICE)
            term = lax.dot_general(a, t, (((0,), (0,)), ((), ())), preferred_element_type=F32)

            @pl.when(i == 0)
            def _(h=h, term=term):
                total[j, h] = term

            @pl.when(i > 0)
            def _(h=h, term=term):
                total[j, h] += term

            if h is not yl:
                for jj in range(blocks):

                    @pl.when((i == PAIRS - 1) & (j == jj))
                    def _(jj=jj):
                        for g, copy in enumerate(out_sends(jj)):
                            half_out[jj, g] = total[jj, 1 - yl, :, g * HB : (g + 1) * HB].astype(BF16)
                            copy.start()

        for jj in range(blocks):

            @pl.when((i == PAIRS - 1) & (j == jj))
            def _(jj=jj):
                for copy in out_copies(jj):
                    copy.start()

        @pl.when(ring(u))
        def _():
            x_sent(u, SCATTER, part.at[u, pl.ds(0, 2)])
            x_sent(u, MIXED, part.at[u, 0])
            x_sent(u, TQ, tq.at[u, :, pl.ds(0, 2)])
            x_sent(u, PASSED, tq.at[u, :, 0])

        @pl.when(u >= units - DIRECT)
        def _():
            x_sent(u, SCATTER, part.at[u, pl.ds(0, 3)])
            x_sent(u, TQ, tq.at[u, :, pl.ds(0, 3)])

    def step(n, carry):
        j, i = place(n)

        def ticks(order):
            if order in (0, 1, 2, 4):

                @pl.when(n < PAIRS // 2)
                def _():
                    tick(AHEAD + 4 * n + min(order, 3))

            if order in (2, 4):
                k = AHEAD + 4 * (PAIRS // 2) + 2 * (n - PAIRS // 2) + (order - 2) // 2

                @pl.when((n >= PAIRS // 2) & (k < TICKS))
                def _():
                    tick(k)

        ticks(0)

        @pl.when((n < 3 * PAIRS // 2) & (j == 0))
        def _():
            c_in((i + 1) % PAIRS).wait_recv()

        for jj in range(blocks):

            @pl.when(n == jj * (PAIRS // 2))
            def _(jj=jj):
                for copy in own_whole(jj):
                    copy.wait()
                for copy in weights_whole(jj, 1 - yl):
                    copy.wait_recv()
                if jj + 1 < blocks:
                    for copy in weight_sends(jj + 1):
                        copy.start()

        for order, (lag, stage) in enumerate(zip(LAGS, (products, mix, hidden, pass_on, finish))):
            if order:
                ticks(order)

            @pl.when((n >= lag) & (n < units + lag))
            def _(lag=lag, stage=stage):
                stage(n - lag)

        return carry

    lax.fori_loop(0, units + LAGS[-1], step, 0)

    parcels_whole.wait_send()
    first_steps, half = tok.at[pl.ds(0, PAIRS - 1), c], tok.at[:, c]
    remote(first_steps, first_steps, z_s.at[0], z_r.at[0, 0, 0, 0], above).wait_send()
    remote(tok.at[0, c, 0], tok.at[0, c, 0], z_last_s.at[0], z_r.at[0, 0, 0, 0], above).wait_send()
    remote(half, half, c_s.at[0], c_r.at[0], other).wait_send()
    for j in range(blocks):
        for copy in weights_whole(j, yl):
            copy.wait_send()
        for copy in out_copies(j):
            copy.wait()
    for j in range(blocks):
        for copy in out_sends(j):
            copy.wait()


def per_device(tokens, w_gate, w_up, probe_gate, probe_up, w_down, out_grad):
    width = w_gate.shape[1]
    blocks = width // HB
    units = blocks * PAIRS
    everywhere = lax.axis_size("dp") * lax.axis_size("fsdp")
    scale = 1.0 / float(tokens.shape[0] * everywhere) ** 0.5
    dma = pltpu.SemaphoreType.DMA
    vmem, any_ = pl.BlockSpec(memory_space=pltpu.VMEM), pl.BlockSpec(memory_space=pl.ANY)
    own_gate, own_up, in_gate, in_up = pl.pallas_call(
        functools.partial(kernel, blocks, scale),
        out_shape=(jax.ShapeDtypeStruct((SLICE, width), F32),) * 2
        + (jax.ShapeDtypeStruct((SLICE, width), BF16),) * 2,
        in_specs=[vmem] + [any_] * 5 + [vmem],
        out_specs=(any_,) * 4,
        scratch_shapes=[
            pltpu.VMEM((16, 8 * SLICE), F32),
            pltpu.VMEM((8, 16, SLICE), BF16),
            pltpu.VMEM((PEERS, 16, SLICE), BF16),
            pltpu.VMEM((PAIRS, 2, 2, 2, CUTS, PIECE, SLICE), BF16),
            pltpu.VMEM((2, blocks, SLICE, 4 * HB), BF16),
            pltpu.VMEM((2, blocks, HB, SLICE), BF16),
            pltpu.VMEM((units, NX, STACK, HB), BF16),
            pltpu.VMEM((units, STACK, HB), BF16),
            pltpu.VMEM((units, STACK, HB), BF16),
            pltpu.VMEM((units, STACK, HB), BF16),
            pltpu.VMEM((units, 2, NX, SHARE, HB), BF16),
            pltpu.VMEM((blocks, 2, SLICE, 2 * HB), F32),
            pltpu.VMEM((blocks, 2, SLICE, HB), BF16),
            dma((1,)),
            dma((1,)),
            dma((1,)),
            dma((1,)),
            dma((PAIRS, 2, 2, CUTS)),
            dma((1,)),
            dma((PAIRS,)),
            dma((blocks, 2)),
            dma((blocks, 2)),
            dma((blocks, 2)),
            dma((SLOTS, 4)),
            dma((SLOTS, 7)),
            dma((blocks, 2)),
            dma((blocks, 2)),
            dma((blocks, 2)),
        ],
        compiler_params=pltpu.CompilerParams(
            collective_id=0, has_side_effects=True, vmem_limit_bytes=62 * 1024 * 1024
        ),
    )(tokens, w_gate, w_up, probe_gate, probe_up, w_down, out_grad)
    return own_gate + in_gate.astype(F32), own_up + in_up.astype(F32)


def solution(mesh):
    placed = (
        P(("dp", "fsdp"), None),
        P("dp", "fsdp"),
        P("dp", "fsdp"),
        P("dp", "fsdp"),
        P("dp", "fsdp"),
        P("fsdp", "dp"),
        P(("dp", "fsdp"), None),
    )
    return jax.shard_map(
        per_device,
        mesh=mesh,
        in_specs=placed,
        out_specs=(P("dp", "fsdp"), P("dp", "fsdp")),
        check_vma=False,
    )
```

```python
import functools

import jax
import jax.numpy as jnp
from jax import lax
from jax.experimental import pallas as pl
from jax.experimental.pallas import tpu as pltpu
from jax.sharding import PartitionSpec as P

MESH = pl.DeviceIdType.MESH
F32, BF16 = jnp.float32, jnp.bfloat16

NX, NY, NZ, NC = 4, 2, 16, 2
PEERS = NX * NY * NC
ROWS = 6
BLOCK = PEERS * ROWS
SLICE = 512
PAIRS = NZ // 2
UNIT = 2 * BLOCK
SHARE = UNIT // NX
STACK = 5 * SHARE
TOP = 128
HB = 128
LAGS = (0, 2, 4, 6, 8)
DIRECT = 1
SLOTS = 10
CUTS = 2
PIECE = BLOCK // CUTS
AHEAD = 4
TICKS = 2 * CUTS * PAIRS


def kernel(
    blocks,
    scale,
    tokens,
    w_gate,
    w_up,
    probe_gate,
    probe_up,
    w_down,
    grads,
    own_gate,
    own_up,
    in_gate,
    in_up,
    both,
    parcels,
    landed,
    tok,
    wide,
    down,
    part,
    via,
    from_left,
    from_right,
    tq,
    total,
    half_out,
    a2a_s,
    a2a_r,
    z_s,
    z_last_s,
    z_r,
    c_s,
    c_r,
    w_l,
    w_s,
    w_r,
    x_s,
    x_r,
    o_s,
    o_r,
    o_l,
):
    dp, fsdp = lax.axis_index("dp"), lax.axis_index("fsdp")
    x, yl = dp // 2, dp % 2
    yh, z, c = fsdp // 32, (fsdp // 2) % NZ, fsdp % 2
    units = blocks * PAIRS

    def device(x_, yl_, yh_, z_, c_):
        return (x_ * 2 + yl_, yh_ * 32 + z_ * 2 + c_)

    xr, xl, xo = (x + 1) % NX, (x + 3) % NX, (x + 2) % NX
    zr, zl = (z + 1) % NZ, (z + NZ - 1) % NZ
    right, left = device(xr, yl, yh, z, c), device(xl, yl, yh, z, c)
    above, below = device(x, yl, yh, zr, c), device(x, yl, yh, zl, c)
    other = device(x, yl, yh, z, 1 - c)
    mate = device(x, 1 - yl, yh, z, c)
    me = x * 4 + yh * 2 + c

    def peer(index):
        return device(index // 4, yl, (index // 2) % 2, z, index % 2)

    def remote(src, dst, send, recv, to):
        return pltpu.make_async_remote_copy(
            src_ref=src, dst_ref=dst, send_sem=send, recv_sem=recv, device_id=to, device_id_type=MESH
        )

    barrier = pltpu.get_barrier_semaphore()

    def greet(k, carry):
        pl.semaphore_signal(barrier, inc=1, device_id=peer((me + k) % PEERS), device_id_type=MESH)
        return carry

    lax.fori_loop(1, PEERS, greet, 0)
    for to in (above, below, mate):
        pl.semaphore_signal(barrier, inc=1, device_id=to, device_id_type=MESH)

    mats = (w_gate, w_up, probe_gate, probe_up)

    def weight_parts(j, slot):
        cols = pl.ds(j * HB, HB)
        pairs = [(m.at[:, cols], wide.at[slot, j, :, pl.ds(i * HB, HB)]) for i, m in enumerate(mats)]
        return pairs + [(w_down.at[cols, :], down.at[slot, j])]

    def own_copies(j):
        return [
            pltpu.make_async_copy(s, d, w_l.at[j, i // 4]) for i, (s, d) in enumerate(weight_parts(j, yl))
        ]

    def weight_sends(j):
        return [
            remote(s, d, w_s.at[j, i // 4], w_r.at[j, i // 4], mate)
            for i, (s, d) in enumerate(weight_parts(j, yl))
        ]

    def weights_whole(j, slot):
        return [
            remote(ref.at[slot, j], ref.at[slot, j], w_s.at[j, i], w_r.at[j, i], mate)
            for i, ref in enumerate((wide, down))
        ]

    def own_whole(j):
        return [
            pltpu.make_async_copy(ref.at[yl, j], ref.at[yl, j], w_l.at[j, i])
            for i, ref in enumerate((wide, down))
        ]

    for j in range(blocks):
        for copy in own_copies(j):
            copy.start()

    values = tokens[...].astype(F32)
    inverse = lax.rsqrt(jnp.mean(values * values, axis=1, keepdims=True) + 1e-05)
    both[...] = jnp.zeros_like(both)
    both[0:ROWS, :] = (values * inverse).astype(BF16).astype(F32)
    both[8 : 8 + ROWS, :] = grads[...].astype(F32)
    for q in range(8):
        parcels[q] = both[:, q * SLICE : (q + 1) * SLICE].astype(BF16)
    landed[me] = parcels[x * 2 + c]

    pl.semaphore_wait(barrier, PEERS - 1 + 3)

    def start_parcel(k, carry):
        to = ((x + (k // 2) % NX) % NX) * 4 + ((yh + 1 + k // 8) % NY) * 2 + (c + k % 2) % NC
        remote(
            parcels.at[(to // 4) * 2 + to % 2], landed.at[me], a2a_s.at[0], a2a_r.at[0], peer(to)
        ).start()
        return carry

    lax.fori_loop(0, PEERS // 2, start_parcel, 0)
    lax.fori_loop(PEERS // 2 + 1, PEERS, start_parcel, 0)
    for copy in weight_sends(0):
        copy.start()
    parcels_whole = remote(
        landed.at[pl.ds(0, PEERS - 1)], landed.at[pl.ds(0, PEERS - 1)], a2a_s.at[0], a2a_r.at[0], other
    )
    parcels_whole.wait_recv()

    col = lax.broadcasted_iota(jnp.int32, (2 * BLOCK, PEERS * 16), 1)
    row = lax.broadcasted_iota(jnp.int32, (2 * BLOCK, PEERS * 16), 0)
    source, place = col >> 4, col & 15
    kind, token = place >> 3, place & 7
    pick = (row == kind * BLOCK + source * ROWS + token) & (token < ROWS)
    packed = jnp.dot(
        jnp.where(pick, 1.0, 0.0).astype(BF16),
        landed[...].reshape(PEERS * 16, SLICE),
        preferred_element_type=F32,
    ).astype(BF16)
    tok[0, c, 0, 0] = packed[:BLOCK].reshape(CUTS, PIECE, SLICE)
    tok[0, c, 1, 0] = packed[BLOCK:].reshape(CUTS, PIECE, SLICE)

    def z_send(s, way, kind, cut):
        src = tok.at[s, c, kind, 0 if isinstance(s, int) else way, cut]
        return remote(
            src, tok.at[s + 1, c, kind, way, cut], z_s.at[0], z_r.at[s + 1, way, kind, cut], (above, below)[way]
        )

    def z_last(way, cut):
        to = device(x, yl, yh, (z + 1 + way * (NZ - 2)) % NZ, c)
        src, dst = tok.at[PAIRS - 1, c, way, way, cut], tok.at[0, c, way, 1, cut]
        return remote(src, dst, z_last_s.at[0], z_r.at[0, 1, way, cut], to)

    def z_in(s, way, kind, cut):
        piece = tok.at[s, c, kind, way, cut]
        return remote(piece, piece, z_s.at[0], z_r.at[s, way, kind, cut], above)

    def c_send(s, way, kind):
        piece = tok.at[s, c, kind, way]
        return remote(piece, piece, c_s.at[0], c_r.at[s], other)

    def c_in(s):
        return remote(tok.at[s, 1 - c], tok.at[s, 1 - c], c_s.at[0], c_r.at[s], other)

    for kind in range(2):
        for cut in range(CUTS):
            for way in range(2):
                z_send(0, way, kind, cut).start()
    for kind in range(2):
        c_send(0, 0, kind).start()

    def tick(k, carry=None):
        s, kind, cut = k // (2 * CUTS) + 1, (k // CUTS) % 2, k % CUTS

        @pl.when(s < PAIRS)
        def _():
            for way in range(2):
                z_in(s, way, kind, cut).wait_recv()

                @pl.when(s < PAIRS - 1)
                def _(way=way):
                    z_send(s, way, kind, cut).start()

            @pl.when(s == PAIRS - 1)
            def _():
                z_last(kind, cut).start()

            @pl.when(cut == CUTS - 1)
            def _():
                for way in range(2):
                    c_send(s, way, kind).start()

        @pl.when(s == PAIRS)
        def _():
            z_in(0, 1, kind, cut).wait_recv()

            @pl.when(cut == CUTS - 1)
            def _():
                c_send(0, 1, kind).start()

        return carry

    lax.fori_loop(0, AHEAD, tick, 0)

    def place(n):
        quarter = n // (PAIRS // 2)
        mixed = ((quarter + 1) // 2) % 2
        last = quarter // 3
        j = mixed * (1 - n % 2) + last
        i = (1 - mixed - last) * n + mixed * (n // 2 - 2 + (n % 2) * 4) + last * (n - PAIRS)
        return j, i

    bottom = STACK - TOP

    F_LEFT, F_RIGHT, LEFT, RIGHT, T_LEFT, T_RIGHT, T_FAR = range(7)
    SCATTER, MIXED, TQ, PASSED = range(4)
    far = device(xo, yl, yh, z, c)

    def x_copy(u, send, recv, src, dst, to):
        slot = u % SLOTS
        return remote(src, dst, x_s.at[slot, send], x_r.at[slot, recv], to)

    def x_start(u, send, *copies):
        for recv, src, dst, to in copies:
            x_copy(u, send, recv, src, dst, to).start()

    def x_wait(u, recv, ref):
        x_copy(u, 0, recv, ref, ref, far).wait_recv()

    def x_sent(u, send, ref):
        x_copy(u, send, 0, ref, ref, far).wait_send()

    top, low = pl.ds(0, TOP), pl.ds(TOP, bottom)

    def ring(u):
        return u < units - DIRECT

    def products(u):
        j, i = place(u)
        s = (i + 1) % PAIRS
        gates = jnp.zeros((UNIT, 4 * HB), F32)
        dhid = jnp.zeros((UNIT, HB), F32)
        for h in range(2):
            a = tok[s, h, 0].reshape(UNIT, SLICE)
            g = tok[s, h, 1].reshape(UNIT, SLICE)
            gates = gates + jnp.dot(a, wide[h, j], preferred_element_type=F32)
            dhid = dhid + lax.dot_general(g, down[h, j], (((1,), (1,)), ((), ())), preferred_element_type=F32)
        for q in range(NX):
            rows = slice(q * SHARE, (q + 1) * SHARE)
            for m in range(4):
                part[u, q, m * SHARE : (m + 1) * SHARE, :] = gates[rows, m * HB : (m + 1) * HB].astype(BF16)
            part[u, q, 4 * SHARE :, :] = (dhid[rows] * scale).astype(BF16)

        x_start(
            u,
            SCATTER,
            (F_LEFT, part.at[u, xo, top], via.at[u, top], right),
            (F_RIGHT, part.at[u, xo, low], via.at[u, low], left),
            (LEFT, part.at[u, xr, low], from_left.at[u, low], right),
            (RIGHT, part.at[u, xl, top], from_right.at[u, top], left),
        )

    def mix(u):
        x_wait(u, F_LEFT, via.at[u, top])
        via[u, :TOP] = (via[u, :TOP].astype(F32) + part[u, xr, :TOP].astype(F32)).astype(BF16)
        x_start(u, MIXED, (LEFT, via.at[u, top], from_left.at[u, top], right))
        x_wait(u, F_RIGHT, via.at[u, low])
        via[u, TOP:] = (via[u, TOP:].astype(F32) + part[u, xl, TOP:].astype(F32)).astype(BF16)
        x_start(u, MIXED, (RIGHT, via.at[u, low], from_right.at[u, low], left))

    def hidden(u):
        x_wait(u, LEFT, from_left.at[u])
        x_wait(u, RIGHT, from_right.at[u])
        stack = part[u, x].astype(F32) + from_left[u].astype(F32) + from_right[u].astype(F32)
        gate, up, tgate, tup, dhid = (stack[m * SHARE : (m + 1) * SHARE] for m in range(5))
        sig = jax.nn.sigmoid(gate)
        first = sig * (1.0 + gate * (1.0 - sig))
        second = sig * (1.0 - sig) * (2.0 + gate * (1.0 - 2.0 * sig))
        tq[u, 0, x] = (dhid * (tup * first + up * second * tgate)).astype(BF16)
        tq[u, 1, x] = (dhid * first * tgate).astype(BF16)
        x_start(
            u,
            TQ,
            (T_LEFT, tq.at[u, :, x], tq.at[u, :, x], right),
            (T_RIGHT, tq.at[u, :, x], tq.at[u, :, x], left),
        )

        @pl.when(u >= units - DIRECT)
        def _():
            x_start(u, TQ, (T_FAR, tq.at[u, :, x], tq.at[u, :, x], far))

    def pass_on(u):
        @pl.when(ring(u))
        def _():
            x_wait(u, T_LEFT, tq.at[u, :, xl])
            x_start(u, PASSED, (T_FAR, tq.at[u, 0, xl], tq.at[u, 0, xl], right))
            x_wait(u, T_RIGHT, tq.at[u, :, xr])
            x_start(u, PASSED, (T_FAR, tq.at[u, 1, xr], tq.at[u, 1, xr], left))

    def out_sends(j):
        cols = pl.ds(j * HB, HB)
        return [
            remote(half_out.at[j, g], ref.at[:, cols], o_s.at[j, g], o_r.at[j, g], mate)
            for g, ref in enumerate((in_gate, in_up))
        ]

    def out_copies(j):
        cols = pl.ds(j * HB, HB)
        return [
            pltpu.make_async_copy(total.at[j, yl, :, pl.ds(g * HB, HB)], ref.at[:, cols], o_l.at[j, g])
            for g, ref in enumerate((own_gate, own_up))
        ]

    def finish(u):
        j, i = place(u)
        s = (i + 1) % PAIRS

        @pl.when(u >= units - DIRECT)
        def _():
            x_wait(u, T_LEFT, tq.at[u, :, xl])
            x_wait(u, T_RIGHT, tq.at[u, :, xr])

        x_wait(u, T_FAR, tq.at[u, :, xo])
        t = jnp.concatenate([tq[u, 0].reshape(UNIT, HB), tq[u, 1].reshape(UNIT, HB)], axis=1)
        for h in (1 - yl, yl):
            a = tok[s, h, 0].reshape(UNIT, SLICE)
            term = lax.dot_general(a, t, (((0,), (0,)), ((), ())), preferred_element_type=F32)

            @pl.when(i == 0)
            def _(h=h, term=term):
                total[j, h] = term

            @pl.when(i > 0)
            def _(h=h, term=term):
                total[j, h] += term

            if h is not yl:
                for jj in range(blocks):

                    @pl.when((i == PAIRS - 1) & (j == jj))
                    def _(jj=jj):
                        for g, copy in enumerate(out_sends(jj)):
                            half_out[jj, g] = total[jj, 1 - yl, :, g * HB : (g + 1) * HB].astype(BF16)
                            copy.start()

        for jj in range(blocks):

            @pl.when((i == PAIRS - 1) & (j == jj))
            def _(jj=jj):
                for copy in out_copies(jj):
                    copy.start()

        x_sent(u, SCATTER, part.at[u, pl.ds(0, 2)])
        x_sent(u, MIXED, part.at[u, 0])

        @pl.when(ring(u))
        def _():
            x_sent(u, TQ, tq.at[u, :, pl.ds(0, 2)])
            x_sent(u, PASSED, tq.at[u, :, 0])

        @pl.when(u >= units - DIRECT)
        def _():
            x_sent(u, TQ, tq.at[u, :, pl.ds(0, 3)])

    def step(n, carry):
        j, i = place(n)

        def ticks(order):
            if order in (0, 1, 2, 4):

                @pl.when(n < PAIRS // 2)
                def _():
                    tick(AHEAD + 4 * n + min(order, 3))

            if order in (2, 4):
                k = AHEAD + 4 * (PAIRS // 2) + 2 * (n - PAIRS // 2) + (order - 2) // 2

                @pl.when((n >= PAIRS // 2) & (k < TICKS))
                def _():
                    tick(k)

        ticks(0)

        @pl.when((n < 3 * PAIRS // 2) & (j == 0))
        def _():
            c_in((i + 1) % PAIRS).wait_recv()

        for jj in range(blocks):

            @pl.when(n == jj * (PAIRS // 2))
            def _(jj=jj):
                for copy in own_whole(jj):
                    copy.wait()
                for copy in weights_whole(jj, 1 - yl):
                    copy.wait_recv()
                if jj + 1 < blocks:
                    for copy in weight_sends(jj + 1):
                        copy.start()

        for order, (lag, stage) in enumerate(zip(LAGS, (products, mix, hidden, pass_on, finish))):
            if order:
                ticks(order)

            @pl.when((n >= lag) & (n < units + lag))
            def _(lag=lag, stage=stage):
                stage(n - lag)

        return carry

    lax.fori_loop(0, units + LAGS[-1], step, 0)

    parcels_whole.wait_send()
    first_steps, half = tok.at[pl.ds(0, PAIRS - 1), c], tok.at[:, c]
    remote(first_steps, first_steps, z_s.at[0], z_r.at[0, 0, 0, 0], above).wait_send()
    remote(tok.at[0, c, 0], tok.at[0, c, 0], z_last_s.at[0], z_r.at[0, 0, 0, 0], above).wait_send()
    remote(half, half, c_s.at[0], c_r.at[0], other).wait_send()
    for j in range(blocks):
        for copy in weights_whole(j, yl):
            copy.wait_send()
        for copy in out_copies(j):
            copy.wait()
    for j in range(blocks):
        for copy in out_sends(j):
            copy.wait()


def per_device(tokens, w_gate, w_up, probe_gate, probe_up, w_down, out_grad):
    width = w_gate.shape[1]
    blocks = width // HB
    units = blocks * PAIRS
    everywhere = lax.axis_size("dp") * lax.axis_size("fsdp")
    scale = 1.0 / float(tokens.shape[0] * everywhere) ** 0.5
    dma = pltpu.SemaphoreType.DMA
    vmem, any_ = pl.BlockSpec(memory_space=pltpu.VMEM), pl.BlockSpec(memory_space=pl.ANY)
    own_gate, own_up, in_gate, in_up = pl.pallas_call(
        functools.partial(kernel, blocks, scale),
        out_shape=(jax.ShapeDtypeStruct((SLICE, width), F32),) * 2
        + (jax.ShapeDtypeStruct((SLICE, width), BF16),) * 2,
        in_specs=[vmem] + [any_] * 5 + [vmem],
        out_specs=(any_,) * 4,
        scratch_shapes=[
            pltpu.VMEM((16, 8 * SLICE), F32),
            pltpu.VMEM((8, 16, SLICE), BF16),
            pltpu.VMEM((PEERS, 16, SLICE), BF16),
            pltpu.VMEM((PAIRS, 2, 2, 2, CUTS, PIECE, SLICE), BF16),
            pltpu.VMEM((2, blocks, SLICE, 4 * HB), BF16),
            pltpu.VMEM((2, blocks, HB, SLICE), BF16),
            pltpu.VMEM((units, NX, STACK, HB), BF16),
            pltpu.VMEM((units, STACK, HB), BF16),
            pltpu.VMEM((units, STACK, HB), BF16),
            pltpu.VMEM((units, STACK, HB), BF16),
            pltpu.VMEM((units, 2, NX, SHARE, HB), BF16),
            pltpu.VMEM((blocks, 2, SLICE, 2 * HB), F32),
            pltpu.VMEM((blocks, 2, SLICE, HB), BF16),
            dma((1,)),
            dma((1,)),
            dma((1,)),
            dma((1,)),
            dma((PAIRS, 2, 2, CUTS)),
            dma((1,)),
            dma((PAIRS,)),
            dma((blocks, 2)),
            dma((blocks, 2)),
            dma((blocks, 2)),
            dma((SLOTS, 4)),
            dma((SLOTS, 7)),
            dma((blocks, 2)),
            dma((blocks, 2)),
            dma((blocks, 2)),
        ],
        compiler_params=pltpu.CompilerParams(
            collective_id=0, has_side_effects=True, vmem_limit_bytes=62 * 1024 * 1024
        ),
    )(tokens, w_gate, w_up, probe_gate, probe_up, w_down, out_grad)
    return own_gate + in_gate.astype(F32), own_up + in_up.astype(F32)


def solution(mesh):
    placed = (
        P(("dp", "fsdp"), None),
        P("dp", "fsdp"),
        P("dp", "fsdp"),
        P("dp", "fsdp"),
        P("dp", "fsdp"),
        P("fsdp", "dp"),
        P(("dp", "fsdp"), None),
    )
    return jax.shard_map(
        per_device,
        mesh=mesh,
        in_specs=placed,
        out_specs=(P("dp", "fsdp"), P("dp", "fsdp")),
        check_vma=False,
    )
```
